128 devices in a mesh: dp: 128 (over y, x, z, core).
Axes of the slice: x: 4, y: 4, z: 4, core: 2. Of those that a mesh axis runs over, the one named last changes fastest.
Arguments:
- img_emb: bfloat16 [65536, 1152], P('dp'), may hold values from -6 to 6
- txt_emb: bfloat16 [65536, 1152], P('dp'), may hold values from -6 to 6
- img_proj: bfloat16 [1152, 1152], replicated, may hold values from -0.1875 to 0.1875
- txt_proj: bfloat16 [1152, 1152], replicated, may hold values from -0.1875 to 0.1875
- log_scale: float32 [1], replicated, may hold values from 1.1 to 2.1
- bias: float32 [1], replicated, may hold values from -3 to -1
Outputs:
- d_img_emb: bfloat16 [65536, 1152], P('dp')
- d_txt_emb: bfloat16 [65536, 1152], P('dp')
- d_img_proj: float32 [1152, 1152], replicated
- d_txt_proj: float32 [1152, 1152], replicated
The draws below stay inside these ranges and needn't reach their ends.
All inputs are finite; a program needn't handle non-finite values.
Results may differ from the reference program's by a relative error of at most 0.02.
Values may be sent and summed in bfloat16 or wider, within the bound.
A program may use at most 128 MiB of HBM per device.

```python
import jax
import jax.numpy as jnp
from jax import lax

D = 1152
ROWS = 512
REACH = 3
TOTAL = 65536
N_DP = 128


def block_scale(key, extent, split, low, high):
    factor_of = 1.0
    for axis_at, blocks in split:
        steps = jax.random.uniform(jax.random.fold_in(jax.random.fold_in(key, 6), axis_at), (blocks,), jnp.float32, low / len(split), high / len(split))
        factor_of = factor_of * jnp.repeat(jnp.exp(steps), extent[axis_at] // blocks).reshape((-1,) + (1,) * (len(extent) - 1 - axis_at))
    return factor_of


def gaussian(stream_key, extent, spread, reach, cuts=(), kind=jnp.bfloat16):
    level = block_scale(stream_key, extent, cuts, -0.22, 0.18) if cuts else 1.0
    values = jax.random.normal(stream_key, extent, jnp.float32) * spread * level
    return jnp.minimum(jnp.maximum(values, -reach), reach).astype(kind)


def setup_inputs(seed: int = 0) -> dict:
    splits = jax.random.split(jax.random.key(seed), 7)
    return {
        "img_emb": gaussian(splits[0], (TOTAL, D), 1.0, 6.0, ((0, 128),)),
        "txt_emb": gaussian(splits[1], (TOTAL, D), 1.0, 6.0, ((0, 128),)),
        "img_proj": gaussian(splits[2], (D, D), D ** -0.5, 0.1875),
        "txt_proj": gaussian(splits[3], (D, D), D ** -0.5, 0.1875),
        "log_scale": jnp.clip(jax.random.uniform(splits[4], (1,), jnp.float32, 1.1, 2.1), 1.1, 2.1),
        "bias": jnp.clip(jax.random.uniform(splits[5], (1,), jnp.float32, -3.0, -1.0), -3.0, -1.0),
    }


def unit_rows(embeddings, projection):
    projected = jnp.dot(embeddings, projection, preferred_element_type=jnp.float32)
    row_norm = jnp.sqrt(lax.optimization_barrier(jnp.sum(projected * projected, axis=1, keepdims=True)) + 1e-06)
    return (projected / row_norm, row_norm)

def unit_back(grad_unit, unit_vals, row_norm):
    inner = lax.optimization_barrier(jnp.sum(unit_vals * grad_unit, axis=1, keepdims=True))
    return (grad_unit - unit_vals * inner) / row_norm

def pair_grads(image_block, text_block, logit_scale, logit_bias, own_block):
    logits = logit_scale * jnp.dot(image_block, text_block.T, preferred_element_type=jnp.float32) + logit_bias
    coefficients = jax.nn.sigmoid(logits)
    if own_block:
        count = logits.shape[0]
        diagonal_mask = jnp.arange(count)[:, None] == jnp.arange(count)[None, :]
        coefficients = jnp.where(diagonal_mask, coefficients - 1.0, coefficients)
    coefficients = coefficients.astype(jnp.bfloat16)
    image_term = logit_scale * jnp.dot(coefficients, text_block, preferred_element_type=jnp.float32)
    text_term = logit_scale * jnp.dot(coefficients.T, image_block, preferred_element_type=jnp.float32)
    return (image_term, text_term)

def reference(img_emb, txt_emb, img_proj, txt_proj, log_scale, bias):
    logit_scale = jnp.exp(log_scale[0])
    logit_bias = bias[0]
    img_unit, img_norm = unit_rows(img_emb, img_proj)
    txt_unit, txt_norm = unit_rows(txt_emb, txt_proj)
    img_blocks = img_unit.astype(jnp.bfloat16).reshape(N_DP, ROWS, D)
    txt_blocks = txt_unit.astype(jnp.bfloat16).reshape(N_DP, ROWS, D)

    def visit_block(text_grads, inputs):
        image_block, block_id = inputs
        image_total = jnp.zeros((ROWS, D), jnp.float32)
        for reach_step in range(-REACH, REACH + 1):
            partner = ((block_id + reach_step) % N_DP).astype(jnp.int32)
            text_block = lax.dynamic_index_in_dim(txt_blocks, partner, 0, keepdims=False)
            image_term, text_term = pair_grads(image_block, text_block, logit_scale, logit_bias, reach_step == 0)
            image_total = image_total + image_term
            current = lax.dynamic_index_in_dim(text_grads, partner, 0, keepdims=False)
            text_grads = lax.dynamic_update_index_in_dim(text_grads, current + text_term, partner, 0)
        return (text_grads, image_total)
    start_grads = jnp.zeros((N_DP, ROWS, D), jnp.float32)
    block_ids = jnp.arange(N_DP, dtype=jnp.int32)
    text_grads, image_grads = lax.scan(visit_block, start_grads, (img_blocks, block_ids))
    grad_img = image_grads.reshape(TOTAL, D)
    grad_txt = text_grads.reshape(TOTAL, D)
    img_du = unit_back(grad_img, img_unit, img_norm).astype(jnp.bfloat16)
    txt_du = unit_back(grad_txt, txt_unit, txt_norm).astype(jnp.bfloat16)
    d_img_emb = jnp.dot(img_du, img_proj.T, preferred_element_type=jnp.float32).astype(jnp.bfloat16)
    d_txt_emb = jnp.dot(txt_du, txt_proj.T, preferred_element_type=jnp.float32).astype(jnp.bfloat16)
    d_img_proj = jnp.dot(img_emb.T, img_du, preferred_element_type=jnp.float32)
    d_txt_proj = jnp.dot(txt_emb.T, txt_du, preferred_element_type=jnp.float32)
    return (d_img_emb, d_txt_emb, d_img_proj, d_txt_proj)
```

```python
import functools

import jax
import jax.numpy as jnp
from jax import lax
from jax.experimental import pallas as pl
from jax.experimental.pallas import tpu as pltpu
from jax.sharding import PartitionSpec as P

MESH = pl.DeviceIdType.MESH
BF = jnp.bfloat16
F32 = jnp.float32

ROWS, D = 512, 1152
CH = 4
CROWS = ROWS // CH
HALF = D // 2
QROWS = HALF // 4
PARTS = 3
PCOLS = D // PARTS
TILES = (QROWS // 16) * (PCOLS // 128)
PIECE = -(-TILES // 4)
OWN, LEFT, RIGHT, PEER, PEER_LEFT, PEER_RIGHT, FAR = range(7)
TO_LEFT, TO_RIGHT, TO_PEER, FWD_LEFT, FWD_RIGHT, RELAY = range(6)

STRIDE = {"y": 32, "x": 8, "z": 2}
AXES = (
    (("y", "x", "z"), ("x", "y", "z"), ("y", "x", "z")),
    (("y", "x", "z"), ("x", "z", "y"), ("z", "y", "x")),
)


def dot(a, b, dims):
    return lax.dot_general(a, b, (dims, ((), ())), preferred_element_type=F32)


def kernel(
    scale_ref, bias_ref, ie_hbm, te_hbm, ip_hbm, tp_hbm,
    die_hbm, dte_hbm, dip_hbm, dtp_hbm,
    emb, proj, z, unit, inv, g, du, demb, dmat, half, r1, p2, r2, x3, a2, full,
    load_sem, out_sem, zs, zr, s0s, s0r, s1s, s1r, s2s, s2r, s3s, s3r, a2s, a2r, a1s, a1r, fs, fr,
):
    me = lax.axis_index("dp")
    core = lax.rem(me, 2)
    chip = lax.div(me, 2)
    at = {
        "z": lax.rem(chip, 4),
        "x": lax.rem(lax.div(chip, 4), 4),
        "y": lax.div(chip, 16),
    }
    peer = me + 1 - 2 * core
    left = lax.rem(me + 126, 128)
    right = lax.rem(me + 2, 128)
    relay_to = lax.rem(me + 127 + 2 * core, 128)

    def axis_peer(axis, d):
        return me + (lax.rem(at[axis] + d, 4) - at[axis]) * STRIDE[axis]

    loads = [
        pltpu.make_async_copy(te_hbm, emb.at[0], load_sem.at[0]),
        pltpu.make_async_copy(tp_hbm, proj.at[0], load_sem.at[1]),
        pltpu.make_async_copy(ie_hbm, emb.at[1], load_sem.at[2]),
        pltpu.make_async_copy(ip_hbm, proj.at[1], load_sem.at[3]),
    ]
    for load in loads:
        load.start()

    barrier = pltpu.get_barrier_semaphore()
    friends = [peer, left, right, relay_to]
    friends += [axis_peer(axis, d) for axis in ("z", "x", "y") for d in (1, 2, 3)]
    for friend in friends:
        pl.semaphore_signal(barrier, inc=1, device_id=(friend,), device_id_type=MESH)

    scale = jnp.exp(jnp.full((1, 1), scale_ref[0], F32))
    shift = jnp.full((1, 1), bias_ref[0], F32)

    started = []

    def send(src, dst, ssem, rsem, device):
        copy = pltpu.make_async_remote_copy(
            src_ref=src, dst_ref=dst, send_sem=ssem, recv_sem=rsem,
            device_id=(device,), device_id_type=MESH,
        )
        copy.start()
        started.append(copy)

    def await_recv(dst, rsem):
        pltpu.make_async_remote_copy(
            src_ref=dst, dst_ref=dst, send_sem=rsem, recv_sem=rsem,
            device_id=(peer,), device_id_type=MESH,
        ).wait_recv()

    def rows_of(c):
        return pl.ds(c * CROWS, CROWS)

    def send_block(side, src_slot, dst_slot, kind, c, device):
        send(
            z.at[side, src_slot, rows_of(c)], z.at[side, dst_slot, rows_of(c)],
            zs.at[side, kind, c], zr.at[side, dst_slot, c], device,
        )

    def await_block(side, slot, c):
        await_recv(z.at[side, slot, rows_of(c)], zr.at[side, slot, c])

    def make_unit(side):
        unit[side] = dot(emb[side], proj[side], ((1,), (0,)))

        def rows(i, _):
            at_rows = pl.ds(pl.multiple_of(i * 32, 32), 32)
            raw = unit[side, at_rows]
            over = 1.0 / jnp.sqrt(jnp.sum(raw * raw, axis=1, keepdims=True) + 1e-6)
            u = raw * over
            unit[side, at_rows] = u
            inv[side, at_rows] = over
            z[side, OWN, at_rows] = u.astype(BF)
            return 0

        lax.fori_loop(0, ROWS // 32, rows, 0)

    def send_own(side):
        for c in range(CH):
            send_block(side, OWN, RIGHT, TO_LEFT, c, left)
            send_block(side, OWN, LEFT, TO_RIGHT, c, right)
        for c in range(CH):
            send_block(side, OWN, PEER, TO_PEER, c, peer)

    def forward(side, c):
        await_block(side, LEFT, c)
        await_block(side, RIGHT, c)
        send_block(side, 2 - core, FAR, RELAY, c, relay_to)
        send_block(side, LEFT, PEER_LEFT, FWD_LEFT, c, peer)
        send_block(side, RIGHT, PEER_RIGHT, FWD_RIGHT, c, peer)

    def pair(side, slot, first, count, own=False, fresh=False):
        block = z[side, slot, pl.ds(first, count)]
        logits = scale * dot(z[1 - side, OWN], block, ((1,), (1,))) + shift
        coef = 1.0 / (1.0 + jnp.exp(-logits))
        if own:
            same = lax.broadcasted_iota(jnp.int32, coef.shape, 0) == (
                lax.broadcasted_iota(jnp.int32, coef.shape, 1) + first
            )
            coef = jnp.where(same, coef - 1.0, coef)
        term = dot(coef.astype(BF), block, ((1,), (0,)))
        g[...] = term if fresh else g[...] + term

    def halves(side, h):
        for slot in (LEFT, RIGHT, PEER_LEFT, PEER_RIGHT):
            if slot in (PEER_LEFT, PEER_RIGHT):
                for c in range(h * CH // 2, (h + 1) * CH // 2):
                    await_block(side, slot, c)
            pair(side, slot, h * ROWS // 2, ROWS // 2)

    def make_du(side):
        def rows(i, _):
            at_rows = pl.ds(pl.multiple_of(i * 32, 32), 32)
            grad = g[at_rows] * scale
            u = unit[side, at_rows]
            inner = jnp.sum(u * grad, axis=1, keepdims=True)
            du[side, at_rows] = ((grad - u * inner) * inv[side, at_rows]).astype(BF)
            return 0

        lax.fori_loop(0, ROWS // 32, rows, 0)

    def make_demb(side, out, sem):
        demb[side] = dot(du[side], proj[side], ((1,), (1,))).astype(BF)
        copy = pltpu.make_async_copy(demb.at[side], out, sem)
        copy.start()
        return copy

    def sum_steps(side, order):
        mine = pl.ds(pl.multiple_of(core * HALF, HALF), HALF)
        theirs = pl.ds(pl.multiple_of((1 - core) * HALF, HALF), HALF)
        cols = [pl.ds(p * PCOLS, PCOLS) for p in range(PARTS)]

        def quarter(i):
            return pl.ds(pl.multiple_of(i * QROWS, QROWS), QROWS)

        def own_rows(i):
            return pl.ds(pl.multiple_of(core * HALF + i * QROWS, QROWS), QROWS)

        def to_peer():
            for p in range(PARTS):
                dmat[side, :, cols[p]] = dot(
                    emb[side], du[side, :, cols[p]], ((0,), (0,))
                ).astype(BF)
                send(
                    dmat.at[side, theirs, cols[p]], half.at[side, :, cols[p]],
                    s0s.at[side, p], s0r.at[side, p], peer,
                )

        def first_axis():
            for p in range(PARTS):
                await_recv(half.at[side, :, cols[p]], s0r.at[side, p])
                half[side, :, cols[p]] = (
                    half[side, :, cols[p]].astype(F32) + dmat[side, mine, cols[p]].astype(F32)
                ).astype(BF)
                axis = order[p][0]
                for d in (1, 2, 3):
                    send(
                        half.at[side, quarter(lax.rem(at[axis] + d, 4)), cols[p]],
                        r1.at[side, p, d - 1],
                        s1s.at[side, p, d - 1], s1r.at[side, p, d - 1], axis_peer(axis, d),
                    )

        def second_axis():
            for p in range(PARTS):
                for d in range(3):
                    await_recv(r1.at[side, p, d], s1r.at[side, p, d])
                total = half[side, quarter(at[order[p][0]]), cols[p]].astype(F32)
                for d in range(3):
                    total = total + r1[side, p, d].astype(F32)
                total = total.astype(BF)
                for t in range(TILES):
                    r, c = divmod(t, PCOLS // 128)
                    p2[side, p, t // PIECE, pl.ds(t % PIECE * 16, 16)] = total[
                        r * 16 : r * 16 + 16, c * 128 : c * 128 + 128
                    ]
                for t in range(TILES, 4 * PIECE):
                    p2[side, p, t // PIECE, pl.ds(t % PIECE * 16, 16)] = jnp.zeros((16, 128), BF)
                axis = order[p][1]
                for d in (1, 2, 3):
                    send(
                        p2.at[side, p, lax.rem(at[axis] + d, 4)], r2.at[side, p, d - 1],
                        s2s.at[side, p, d - 1], s2r.at[side, p, d - 1], axis_peer(axis, d),
                    )

        def third_axis():
            for p in range(PARTS):
                for d in range(3):
                    await_recv(r2.at[side, p, d], s2r.at[side, p, d])
                total = p2[side, p, at[order[p][1]]].astype(F32)
                for d in range(3):
                    total = total + r2[side, p, d].astype(F32)
                axis = order[p][2]
                x3[side, p, at[axis]] = total.astype(BF)
                for d in (1, 2, 3):
                    send(
                        x3.at[side, p, at[axis]], x3.at[side, p, at[axis]],
                        s3s.at[side, p, d - 1], s3r.at[side, p, d - 1], axis_peer(axis, d),
                    )

        def second_back():
            for p in range(PARTS):
                axis = order[p][2]
                for d in (1, 2, 3):
                    await_recv(x3.at[side, p, lax.rem(at[axis] + 4 - d, 4)], s3r.at[side, p, d - 1])
                total = x3[side, p, 0].astype(F32)
                for i in (1, 2, 3):
                    total = total + x3[side, p, i].astype(F32)
                axis = order[p][1]
                a2[side, p, at[axis]] = total.astype(BF)
                for d in (1, 2, 3):
                    send(
                        a2.at[side, p, at[axis]], a2.at[side, p, at[axis]],
                        a2s.at[side, p, d - 1], a2r.at[side, p, d - 1], axis_peer(axis, d),
                    )

        def first_back():
            for p in range(PARTS):
                axis = order[p][1]
                for d in (1, 2, 3):
                    await_recv(a2.at[side, p, lax.rem(at[axis] + 4 - d, 4)], a2r.at[side, p, d - 1])
                axis = order[p][0]
                for t in range(TILES):
                    r, c = divmod(t, PCOLS // 128)
                    full[
                        side,
                        pl.ds(pl.multiple_of(core * HALF + at[axis] * QROWS + r * 16, 16), 16),
                        pl.ds(p * PCOLS + c * 128, 128),
                    ] = a2[side, p, t // PIECE, pl.ds(t % PIECE * 16, 16)]
                piece = full.at[side, own_rows(at[axis]), cols[p]]
                for d in (1, 2, 3):
                    send(piece, piece, a1s.at[side, p, d - 1], a1r.at[side, p, d - 1], axis_peer(axis, d))
                send(piece, piece, fs.at[side, p, 0], fr.at[side, p, 0], peer)

        def peer_back():
            for p in range(PARTS):
                axis = order[p][0]
                for d in (1, 2, 3):
                    piece = full.at[side, own_rows(lax.rem(at[axis] + 4 - d, 4)), cols[p]]
                    await_recv(piece, a1r.at[side, p, d - 1])
                    send(piece, piece, fs.at[side, p, d], fr.at[side, p, d], peer)

        def finish():
            for p in range(PARTS):
                axis = order[p][0]
                for d in range(4):
                    piece = full.at[
                        side,
                        pl.ds(
                            pl.multiple_of(
                                (1 - core) * HALF + lax.rem(at[axis] + 4 - d, 4) * QROWS, QROWS
                            ),
                            QROWS,
                        ),
                        cols[p],
                    ]
                    await_recv(piece, fr.at[side, p, d])

        return [
            to_peer, first_axis, second_axis, third_axis, second_back, first_back, peer_back, finish
        ]

    loads[0].wait()
    loads[1].wait()
    make_unit(0)
    pl.semaphore_wait(barrier, len(friends))
    send_own(0)
    loads[2].wait()
    loads[3].wait()
    make_unit(1)

    outs = []
    steps = []
    for side in (0, 1):
        def step():
            if steps:
                steps.pop(0)()

        for h in (0, 1):
            pair(side, OWN, h * ROWS // 2, ROWS // 2, own=True, fresh=h == 0)
        step()
        for c in range(CH):
            await_block(side, PEER, c)
        pair(side, PEER, 0, ROWS)
        step()
        for h in (0, 1):
            for c in range(h * CH // 2, (h + 1) * CH // 2):
                forward(side, c)
                step()
            if h == 1 and side == 0:
                send_own(1)
            halves(side, h)
            step()
        for c in range(CH):
            await_block(side, FAR, c)
        pair(side, FAR, 0, ROWS)
        while steps:
            step()
        target = 1 - side
        make_du(target)
        order = AXES[side]
        steps = sum_steps(target, order)
        steps.pop(0)()
        outs.append(make_demb(target, (die_hbm, dte_hbm)[side], out_sem.at[side]))
        if side == 1:
            outs.append(pltpu.make_async_copy(full.at[1], dip_hbm, out_sem.at[2]))
            outs[-1].start()
    while steps:
        steps.pop(0)()
    outs.append(pltpu.make_async_copy(full.at[0], dtp_hbm, out_sem.at[3]))
    outs[-1].start()
    for out in outs:
        out.wait()
    for copy in started:
        copy.wait_send()


def body(img_emb, txt_emb, img_proj, txt_proj, log_scale, bias):
    any_space = pl.BlockSpec(memory_space=pl.ANY)
    smem = pl.BlockSpec(memory_space=pltpu.SMEM)
    dma = pltpu.SemaphoreType.DMA
    d_img_emb, d_txt_emb, d_img_proj, d_txt_proj = pl.pallas_call(
        kernel,
        out_shape=(
            jax.ShapeDtypeStruct((ROWS, D), BF),
            jax.ShapeDtypeStruct((ROWS, D), BF),
            jax.ShapeDtypeStruct((D, D), BF),
            jax.ShapeDtypeStruct((D, D), BF),
        ),
        in_specs=[smem, smem] + [any_space] * 4,
        out_specs=(any_space,) * 4,
        scratch_shapes=[
            pltpu.VMEM((2, ROWS, D), BF),
            pltpu.VMEM((2, D, D), BF),
            pltpu.VMEM((2, 7, ROWS, D), BF),
            pltpu.VMEM((2, ROWS, D), F32),
            pltpu.VMEM((2, ROWS, 1), F32),
            pltpu.VMEM((ROWS, D), F32),
            pltpu.VMEM((2, ROWS, D), BF),
            pltpu.VMEM((2, ROWS, D), BF),
            pltpu.VMEM((2, D, D), BF),
            pltpu.VMEM((2, HALF, D), BF),
            pltpu.VMEM((2, PARTS, 3, QROWS, PCOLS), BF),
            pltpu.VMEM((2, PARTS, 4, PIECE * 16, 128), BF),
            pltpu.VMEM((2, PARTS, 3, PIECE * 16, 128), BF),
            pltpu.VMEM((2, PARTS, 4, PIECE * 16, 128), BF),
            pltpu.VMEM((2, PARTS, 4, PIECE * 16, 128), BF),
            pltpu.VMEM((2, D, D), BF),
            dma((4,)), dma((4,)),
            dma((2, 6, CH)), dma((2, 7, CH)),
            dma((2, PARTS)), dma((2, PARTS)),
            dma((2, PARTS, 3)), dma((2, PARTS, 3)),
            dma((2, PARTS, 3)), dma((2, PARTS, 3)),
            dma((2, PARTS, 3)), dma((2, PARTS, 3)),
            dma((2, PARTS, 3)), dma((2, PARTS, 3)),
            dma((2, PARTS, 3)), dma((2, PARTS, 3)),
            dma((2, PARTS, 4)), dma((2, PARTS, 4)),
        ],
        compiler_params=pltpu.CompilerParams(
            collective_id=0, has_side_effects=True, vmem_limit_bytes=62 << 20
        ),
        name="band_gradients",
    )(log_scale, bias, img_emb, txt_emb, img_proj, txt_proj)
    return (d_img_emb, d_txt_emb, d_img_proj.astype(F32), d_txt_proj.astype(F32))


def solution(mesh):
    return jax.shard_map(
        body,
        mesh=mesh,
        in_specs=(P("dp", None), P("dp", None), P(), P(), P(), P()),
        out_specs=(P("dp", None), P("dp", None), P(), P()),
        check_vma=False,
    )
```

```python
import functools

import jax
import jax.numpy as jnp
from jax import lax
from jax.experimental import pallas as pl
from jax.experimental.pallas import tpu as pltpu
from jax.sharding import PartitionSpec as P

MESH = pl.DeviceIdType.MESH
BF = jnp.bfloat16
F32 = jnp.float32

ROWS, D = 512, 1152
CH = 4
CROWS = ROWS // CH
HALF = D // 2
QROWS = HALF // 4
PARTS = 3
PCOLS = D // PARTS
TILES = (QROWS // 16) * (PCOLS // 128)
PIECE = -(-TILES // 4)
OWN, LEFT, RIGHT, PEER, PEER_LEFT, PEER_RIGHT, FAR = range(7)
TO_LEFT, TO_RIGHT, TO_PEER, FWD_LEFT, FWD_RIGHT, RELAY = range(6)

STRIP = 128

STRIDE = {"y": 32, "x": 8, "z": 2}
AXES = (
    (("y", "x", "z"), ("x", "z", "y"), ("z", "y", "x")),
    (("y", "x", "z"), ("x", "z", "y"), ("z", "y", "x")),
)


def dot(a, b, dims):
    return lax.dot_general(a, b, (dims, ((), ())), preferred_element_type=F32)


def kernel(
    scale_ref, bias_ref, ie_hbm, te_hbm, ip_hbm, tp_hbm,
    die_hbm, dte_hbm, dip_hbm, dtp_hbm,
    emb, proj, z, unit, inv, g, du, demb, dmat, half, r1, p2, r2, x3, a2, full,
    load_sem, out_sem, zs, zr, s0s, s0r, s1s, s1r, s2s, s2r, s3s, s3r, a2s, a2r, a1s, a1r, fs, fr,
):
    me = lax.axis_index("dp")
    core = lax.rem(me, 2)
    chip = lax.div(me, 2)
    at = {
        "z": lax.rem(chip, 4),
        "x": lax.rem(lax.div(chip, 4), 4),
        "y": lax.div(chip, 16),
    }
    peer = me + 1 - 2 * core
    left = lax.rem(me + 126, 128)
    right = lax.rem(me + 2, 128)
    relay_to = lax.rem(me + 127 + 2 * core, 128)

    def axis_peer(axis, d):
        return me + (lax.rem(at[axis] + d, 4) - at[axis]) * STRIDE[axis]

    loads = [
        pltpu.make_async_copy(te_hbm, emb.at[0], load_sem.at[0]),
        pltpu.make_async_copy(tp_hbm, proj.at[0], load_sem.at[1]),
        pltpu.make_async_copy(ie_hbm, emb.at[1], load_sem.at[2]),
        pltpu.make_async_copy(ip_hbm, proj.at[1], load_sem.at[3]),
    ]
    for load in loads[:2]:
        load.start()

    barrier = pltpu.get_barrier_semaphore()
    friends = [peer, left, right, relay_to]
    friends += [axis_peer(axis, d) for axis in ("z", "x", "y") for d in (1, 2, 3)]
    for friend in friends:
        pl.semaphore_signal(barrier, inc=1, device_id=(friend,), device_id_type=MESH)

    scale = jnp.exp(jnp.full((1, 1), scale_ref[0], F32))
    shift = jnp.full((1, 1), bias_ref[0], F32)

    started = []

    def send(src, dst, ssem, rsem, device):
        copy = pltpu.make_async_remote_copy(
            src_ref=src, dst_ref=dst, send_sem=ssem, recv_sem=rsem,
            device_id=(device,), device_id_type=MESH,
        )
        copy.start()
        started.append(copy)

    def await_recv(dst, rsem):
        pltpu.make_async_remote_copy(
            src_ref=dst, dst_ref=dst, send_sem=rsem, recv_sem=rsem,
            device_id=(peer,), device_id_type=MESH,
        ).wait_recv()

    def rows_of(c):
        return pl.ds(c * CROWS, CROWS)

    def send_block(side, src_slot, dst_slot, kind, c, device):
        send(
            z.at[side, src_slot, rows_of(c)], z.at[side, dst_slot, rows_of(c)],
            zs.at[side, kind, c], zr.at[side, dst_slot, c], device,
        )

    def await_block(side, slot, c):
        await_recv(z.at[side, slot, rows_of(c)], zr.at[side, slot, c])

    def make_unit(side, first=0, count=ROWS):
        some = pl.ds(first, count)
        unit[side, some] = dot(emb[side, some], proj[side], ((1,), (0,)))

        def rows(i, _):
            at_rows = pl.ds(pl.multiple_of(first + i * STRIP, STRIP), STRIP)
            raw = unit[side, at_rows]
            over = lax.rsqrt(jnp.sum(raw * raw, axis=1, keepdims=True) + 1e-6)
            u = raw * over
            unit[side, at_rows] = u
            inv[side, at_rows] = over
            z[side, OWN, at_rows] = u.astype(BF)
            return 0

        lax.fori_loop(0, count // STRIP, rows, 0)

    def send_own(side, c):
        send_block(side, OWN, RIGHT, TO_LEFT, c, left)
        send_block(side, OWN, LEFT, TO_RIGHT, c, right)
        send_block(side, OWN, PEER, TO_PEER, c, peer)

    def forward(side, c):
        await_block(side, LEFT, c)
        await_block(side, RIGHT, c)
        send_block(side, 2 - core, FAR, RELAY, c, relay_to)
        send_block(side, LEFT, PEER_LEFT, FWD_LEFT, c, peer)
        send_block(side, RIGHT, PEER_RIGHT, FWD_RIGHT, c, peer)

    def pair(side, slot, first, count, own=False, fresh=False):
        block = z[side, slot, pl.ds(first, count)]
        logits = scale * dot(z[1 - side, OWN], block, ((1,), (1,))) + shift
        coef = 1.0 / (1.0 + jnp.exp(-logits))
        if own:
            same = lax.broadcasted_iota(jnp.int32, coef.shape, 0) == (
                lax.broadcasted_iota(jnp.int32, coef.shape, 1) + first
            )
            coef = jnp.where(same, coef - 1.0, coef)
        term = dot(coef.astype(BF), block, ((1,), (0,)))
        g[...] = term if fresh else g[...] + term

    def halves(side, h):
        for slot in (LEFT, RIGHT, PEER_LEFT, PEER_RIGHT):
            if slot in (PEER_LEFT, PEER_RIGHT):
                for c in range(h * CH // 2, (h + 1) * CH // 2):
                    await_block(side, slot, c)
            pair(side, slot, h * ROWS // 2, ROWS // 2)

    def make_du(side):
        def rows(i, _):
            at_rows = pl.ds(pl.multiple_of(i * STRIP, STRIP), STRIP)
            grad = g[at_rows] * scale
            u = unit[side, at_rows]
            inner = jnp.sum(u * grad, axis=1, keepdims=True)
            du[side, at_rows] = ((grad - u * inner) * inv[side, at_rows]).astype(BF)
            return 0

        lax.fori_loop(0, ROWS // STRIP, rows, 0)

    def make_demb(side, out, sem):
        demb[side] = dot(du[side], proj[side], ((1,), (1,))).astype(BF)
        copy = pltpu.make_async_copy(demb.at[side], out, sem)
        copy.start()
        return copy

    def sum_steps(side, order):
        mine = pl.ds(pl.multiple_of(core * HALF, HALF), HALF)
        theirs = pl.ds(pl.multiple_of((1 - core) * HALF, HALF), HALF)
        cols = [pl.ds(p * PCOLS, PCOLS) for p in range(PARTS)]

        def quarter(i):
            return pl.ds(pl.multiple_of(i * QROWS, QROWS), QROWS)

        def own_rows(i):
            return pl.ds(pl.multiple_of(core * HALF + i * QROWS, QROWS), QROWS)

        def to_peer():
            for p in range(PARTS):
                dmat[side, :, cols[p]] = dot(
                    emb[side], du[side, :, cols[p]], ((0,), (0,))
                ).astype(BF)
                send(
                    dmat.at[side, theirs, cols[p]], half.at[side, :, cols[p]],
                    s0s.at[side, p], s0r.at[side, p], peer,
                )

        def first_axis():
            for p in range(PARTS):
                await_recv(half.at[side, :, cols[p]], s0r.at[side, p])
                half[side, :, cols[p]] = (
                    half[side, :, cols[p]].astype(F32) + dmat[side, mine, cols[p]].astype(F32)
                ).astype(BF)
                axis = order[p][0]
                for d in (1, 2, 3):
                    send(
                        half.at[side, quarter(lax.rem(at[axis] + d, 4)), cols[p]],
                        r1.at[side, p, d - 1],
                        s1s.at[side, p, d - 1], s1r.at[side, p, d - 1], axis_peer(axis, d),
                    )

        def second_axis():
            for p in range(PARTS):
                for d in range(3):
                    await_recv(r1.at[side, p, d], s1r.at[side, p, d])
                total = half[side, quarter(at[order[p][0]]), cols[p]].astype(F32)
                for d in range(3):
                    total = total + r1[side, p, d].astype(F32)
                total = total.astype(BF)
                for t in range(TILES):
                    r, c = divmod(t, PCOLS // 128)
                    p2[side, p, t // PIECE, pl.ds(t % PIECE * 16, 16)] = total[
                        r * 16 : r * 16 + 16, c * 128 : c * 128 + 128
                    ]
                for t in range(TILES, 4 * PIECE):
                    p2[side, p, t // PIECE, pl.ds(t % PIECE * 16, 16)] = jnp.zeros((16, 128), BF)
                axis = order[p][1]
                for d in (1, 2, 3):
                    send(
                        p2.at[side, p, lax.rem(at[axis] + d, 4)], r2.at[side, p, d - 1],
                        s2s.at[side, p, d - 1], s2r.at[side, p, d - 1], axis_peer(axis, d),
                    )

        def third_axis():
            for p in range(PARTS):
                for d in range(3):
                    await_recv(r2.at[side, p, d], s2r.at[side, p, d])
                total = p2[side, p, at[order[p][1]]].astype(F32)
                for d in range(3):
                    total = total + r2[side, p, d].astype(F32)
                axis = order[p][2]
                x3[side, p, at[axis]] = total.astype(BF)
                for d in (1, 2, 3):
                    send(
                        x3.at[side, p, at[axis]], x3.at[side, p, at[axis]],
                        s3s.at[side, p, d - 1], s3r.at[side, p, d - 1], axis_peer(axis, d),
                    )

        def second_back():
            for p in range(PARTS):
                axis = order[p][2]
                for d in (1, 2, 3):
                    await_recv(x3.at[side, p, lax.rem(at[axis] + 4 - d, 4)], s3r.at[side, p, d - 1])
                total = x3[side, p, 0].astype(F32)
                for i in (1, 2, 3):
                    total = total + x3[side, p, i].astype(F32)
                axis = order[p][1]
                a2[side, p, at[axis]] = total.astype(BF)
                for d in (1, 2, 3):
                    send(
                        a2.at[side, p, at[axis]], a2.at[side, p, at[axis]],
                        a2s.at[side, p, d - 1], a2r.at[side, p, d - 1], axis_peer(axis, d),
                    )

        def first_back():
            for p in range(PARTS):
                axis = order[p][1]
                for d in (1, 2, 3):
                    await_recv(a2.at[side, p, lax.rem(at[axis] + 4 - d, 4)], a2r.at[side, p, d - 1])
                axis = order[p][0]
                for t in range(TILES):
                    r, c = divmod(t, PCOLS // 128)
                    full[
                        side,
                        pl.ds(pl.multiple_of(core * HALF + at[axis] * QROWS + r * 16, 16), 16),
                        pl.ds(p * PCOLS + c * 128, 128),
                    ] = a2[side, p, t // PIECE, pl.ds(t % PIECE * 16, 16)]
                piece = full.at[side, own_rows(at[axis]), cols[p]]
                for d in (1, 2, 3):
                    send(piece, piece, a1s.at[side, p, d - 1], a1r.at[side, p, d - 1], axis_peer(axis, d))
                send(piece, piece, fs.at[side, p, 0], fr.at[side, p, 0], peer)

        def peer_back():
            for p in range(PARTS):
                axis = order[p][0]
                for d in (1, 2, 3):
                    piece = full.at[side, own_rows(lax.rem(at[axis] + 4 - d, 4)), cols[p]]
                    await_recv(piece, a1r.at[side, p, d - 1])
                    send(piece, piece, fs.at[side, p, d], fr.at[side, p, d], peer)

        def finish():
            for p in range(PARTS):
                axis = order[p][0]
                for d in range(4):
                    piece = full.at[
                        side,
                        pl.ds(
                            pl.multiple_of(
                                (1 - core) * HALF + lax.rem(at[axis] + 4 - d, 4) * QROWS, QROWS
                            ),
                            QROWS,
                        ),
                        cols[p],
                    ]
                    await_recv(piece, fr.at[side, p, d])

        return [
            to_peer, first_axis, second_axis, third_axis, second_back, first_back, peer_back, finish
        ]

    loads[0].wait()
    loads[1].wait()
    for load in loads[2:]:
        load.start()
    for h in (0, 1):
        make_unit(0, h * ROWS // 2, ROWS // 2)
        if h == 0:
            pl.semaphore_wait(barrier, len(friends))
        for c in range(h * CH // 2, (h + 1) * CH // 2):
            send_own(0, c)
    loads[2].wait()
    loads[3].wait()
    make_unit(1)

    def finish_side(side):
        target = 1 - side
        make_du(target)
        steps = sum_steps(target, AXES[side])
        steps[0]()
        return steps

    def put_demb(side):
        outs.append(make_demb(1 - side, (die_hbm, dte_hbm)[side], out_sem.at[side]))

    def own_pair(side):
        for h in (0, 1):
            pair(side, OWN, h * ROWS // 2, ROWS // 2, own=True, fresh=h == 0)

    def peer_pair(side):
        for c in range(CH):
            await_block(side, PEER, c)
        pair(side, PEER, 0, ROWS)

    def far_pair(side):
        for h in (0, 1):
            for c in range(h * CH // 2, (h + 1) * CH // 2):
                await_block(side, FAR, c)
            pair(side, FAR, h * ROWS // 2, ROWS // 2)

    def put_out(target, out, sem):
        outs.append(pltpu.make_async_copy(full.at[target], out, sem))
        outs[-1].start()

    outs = []
    own_pair(0)
    peer_pair(0)
    forward(0, 0)
    forward(0, 1)
    halves(0, 0)
    forward(0, 2)
    forward(0, 3)
    for c in range(CH):
        send_own(1, c)
    halves(0, 1)
    far_pair(0)
    image = finish_side(0)
    own_pair(1)
    peer_pair(1)
    put_demb(0)
    forward(1, 0)
    forward(1, 1)
    forward(1, 2)
    forward(1, 3)
    image[1]()
    halves(1, 0)
    halves(1, 1)
    far_pair(1)
    text = finish_side(1)
    image[2]()
    text[1]()
    put_demb(1)
    image[3]()
    text[2]()
    image[4]()
    text[3]()
    image[5]()
    text[4]()
    image[6]()
    text[5]()
    image[7]()
    put_out(1, dip_hbm, out_sem.at[2])
    text[6]()
    text[7]()
    put_out(0, dtp_hbm, out_sem.at[3])
    for out in outs:
        out.wait()
    for copy in started:
        copy.wait_send()


def finish_kernel(ie, te, ip, tp, out_ie, out_te, out_ip, out_tp):
    out_ie[...] = ie[...]
    out_te[...] = te[...]
    out_ip[...] = ip[...].astype(F32)
    out_tp[...] = tp[...].astype(F32)


def finish(*parts):
    steps = 4

    def spec(rows):
        return pl.BlockSpec((rows // steps, D), lambda i: (i, 0))

    specs = (spec(ROWS), spec(ROWS), spec(D), spec(D))
    return pl.pallas_call(
        finish_kernel,
        grid=(steps,),
        out_shape=tuple(
            jax.ShapeDtypeStruct((n, D), kind) for n, kind in ((ROWS, BF), (ROWS, BF), (D, F32), (D, F32))
        ),
        in_specs=list(specs),
        out_specs=specs,
        compiler_params=pltpu.CompilerParams(vmem_limit_bytes=62 << 20),
        name="finish",
    )(*parts)


def body(img_emb, txt_emb, img_proj, txt_proj, log_scale, bias):
    any_space = pl.BlockSpec(memory_space=pl.ANY)
    smem = pl.BlockSpec(memory_space=pltpu.SMEM)
    dma = pltpu.SemaphoreType.DMA
    d_img_emb, d_txt_emb, d_img_proj, d_txt_proj = pl.pallas_call(
        kernel,
        out_shape=(
            jax.ShapeDtypeStruct((ROWS, D), BF),
            jax.ShapeDtypeStruct((ROWS, D), BF),
            jax.ShapeDtypeStruct((D, D), BF),
            jax.ShapeDtypeStruct((D, D), BF),
        ),
        in_specs=[smem, smem] + [any_space] * 4,
        out_specs=(any_space,) * 4,
        scratch_shapes=[
            pltpu.VMEM((2, ROWS, D), BF),
            pltpu.VMEM((2, D, D), BF),
            pltpu.VMEM((2, 7, ROWS, D), BF),
            pltpu.VMEM((2, ROWS, D), F32),
            pltpu.VMEM((2, ROWS, 1), F32),
            pltpu.VMEM((ROWS, D), F32),
            pltpu.VMEM((2, ROWS, D), BF),
            pltpu.VMEM((2, ROWS, D), BF),
            pltpu.VMEM((2, D, D), BF),
            pltpu.VMEM((2, HALF, D), BF),
            pltpu.VMEM((2, PARTS, 3, QROWS, PCOLS), BF),
            pltpu.VMEM((2, PARTS, 4, PIECE * 16, 128), BF),
            pltpu.VMEM((2, PARTS, 3, PIECE * 16, 128), BF),
            pltpu.VMEM((2, PARTS, 4, PIECE * 16, 128), BF),
            pltpu.VMEM((2, PARTS, 4, PIECE * 16, 128), BF),
            pltpu.VMEM((2, D, D), BF),
            dma((4,)), dma((4,)),
            dma((2, 6, CH)), dma((2, 7, CH)),
            dma((2, PARTS)), dma((2, PARTS)),
            dma((2, PARTS, 3)), dma((2, PARTS, 3)),
            dma((2, PARTS, 3)), dma((2, PARTS, 3)),
            dma((2, PARTS, 3)), dma((2, PARTS, 3)),
            dma((2, PARTS, 3)), dma((2, PARTS, 3)),
            dma((2, PARTS, 3)), dma((2, PARTS, 3)),
            dma((2, PARTS, 4)), dma((2, PARTS, 4)),
        ],
        compiler_params=pltpu.CompilerParams(
            collective_id=0, has_side_effects=True, vmem_limit_bytes=62 << 20
        ),
        name="band_gradients",
    )(log_scale, bias, img_emb, txt_emb, img_proj, txt_proj)
    return finish(d_img_emb, d_txt_emb, d_img_proj, d_txt_proj)


def solution(mesh):
    return jax.shard_map(
        body,
        mesh=mesh,
        in_specs=(P("dp", None), P("dp", None), P(), P(), P(), P()),
        out_specs=(P("dp", None), P("dp", None), P(), P()),
        check_vma=False,
    )
```

```python
import functools

import jax
import jax.numpy as jnp
from jax import lax
from jax.experimental import pallas as pl
from jax.experimental.pallas import tpu as pltpu
from jax.sharding import PartitionSpec as P

MESH = pl.DeviceIdType.MESH
BF = jnp.bfloat16
F32 = jnp.float32

ROWS, D = 512, 1152
CH = 4
CROWS = ROWS // CH
HALF = D // 2
QROWS = HALF // 4
PARTS = 3
PCOLS = D // PARTS
TILES = (QROWS // 16) * (PCOLS // 128)
PIECE = -(-TILES // 4)
OWN, LEFT, RIGHT, PEER, PEER_LEFT, PEER_RIGHT, FAR = range(7)
TO_LEFT, TO_RIGHT, TO_PEER, FWD_LEFT, FWD_RIGHT, RELAY = range(6)

STRIP = 128
PIECE_ROWS = 288

STRIDE = {"y": 32, "x": 8, "z": 2}
AXES = (
    (("y", "x", "z"), ("x", "z", "y"), ("z", "y", "x")),
    (("y", "x", "z"), ("x", "z", "y"), ("z", "y", "x")),
)


def dot(a, b, dims):
    return lax.dot_general(a, b, (dims, ((), ())), preferred_element_type=F32)


def kernel(
    scale_ref, bias_ref, ie_hbm, te_hbm, ip_hbm, tp_hbm,
    die_hbm, dte_hbm, dip_hbm, dtp_hbm,
    emb, proj, z, unit, inv, g, du, demb, dmat, half, r1, p2, r2, x3, a2, full,
    load_sem, out_sem, zs, zr, s0s, s0r, s1s, s1r, s2s, s2r, s3s, s3r, a2s, a2r, a1s, a1r, fs, fr,
):
    me = lax.axis_index("dp")
    core = lax.rem(me, 2)
    chip = lax.div(me, 2)
    at = {
        "z": lax.rem(chip, 4),
        "x": lax.rem(lax.div(chip, 4), 4),
        "y": lax.div(chip, 16),
    }
    peer = me + 1 - 2 * core
    left = lax.rem(me + 126, 128)
    right = lax.rem(me + 2, 128)
    relay_to = lax.rem(me + 127 + 2 * core, 128)

    def axis_peer(axis, d):
        return me + (lax.rem(at[axis] + d, 4) - at[axis]) * STRIDE[axis]

    loads = [
        pltpu.make_async_copy(te_hbm, emb.at[0], load_sem.at[0]),
        pltpu.make_async_copy(tp_hbm, proj.at[0], load_sem.at[1]),
        pltpu.make_async_copy(ie_hbm, emb.at[1], load_sem.at[2]),
        pltpu.make_async_copy(ip_hbm, proj.at[1], load_sem.at[3]),
    ]
    for load in loads[:2]:
        load.start()

    barrier = pltpu.get_barrier_semaphore()
    friends = [peer, left, right, relay_to]
    friends += [axis_peer(axis, d) for axis in ("z", "x", "y") for d in (1, 2, 3)]
    for friend in friends:
        pl.semaphore_signal(barrier, inc=1, device_id=(friend,), device_id_type=MESH)

    scale = jnp.exp(jnp.full((1, 1), scale_ref[0], F32))
    shift = jnp.full((1, 1), bias_ref[0], F32)

    started = []

    def send(src, dst, ssem, rsem, device):
        copy = pltpu.make_async_remote_copy(
            src_ref=src, dst_ref=dst, send_sem=ssem, recv_sem=rsem,
            device_id=(device,), device_id_type=MESH,
        )
        copy.start()
        started.append(copy)

    def await_recv(dst, rsem):
        pltpu.make_async_remote_copy(
            src_ref=dst, dst_ref=dst, send_sem=rsem, recv_sem=rsem,
            device_id=(peer,), device_id_type=MESH,
        ).wait_recv()

    def rows_of(c):
        return pl.ds(c * CROWS, CROWS)

    def send_block(side, src_slot, dst_slot, kind, c, device):
        send(
            z.at[side, src_slot, rows_of(c)], z.at[side, dst_slot, rows_of(c)],
            zs.at[side, kind, c], zr.at[side, dst_slot, c], device,
        )

    def await_block(side, slot, c):
        await_recv(z.at[side, slot, rows_of(c)], zr.at[side, slot, c])

    def make_unit(side, first=0, count=ROWS):
        some = pl.ds(first, count)
        unit[side, some] = dot(emb[side, some], proj[side], ((1,), (0,)))

        def rows(i, _):
            at_rows = pl.ds(pl.multiple_of(first + i * STRIP, STRIP), STRIP)
            raw = unit[side, at_rows]
            over = lax.rsqrt(jnp.sum(raw * raw, axis=1, keepdims=True) + 1e-6)
            u = raw * over
            unit[side, at_rows] = u
            inv[side, at_rows] = over
            z[side, OWN, at_rows] = u.astype(BF)
            return 0

        lax.fori_loop(0, count // STRIP, rows, 0)

    def send_own(side, c):
        send_block(side, OWN, RIGHT, TO_LEFT, c, left)
        send_block(side, OWN, LEFT, TO_RIGHT, c, right)
        send_block(side, OWN, PEER, TO_PEER, c, peer)

    def forward(side, c):
        await_block(side, LEFT, c)
        await_block(side, RIGHT, c)
        send_block(side, 2 - core, FAR, RELAY, c, relay_to)
        send_block(side, LEFT, PEER_LEFT, FWD_LEFT, c, peer)
        send_block(side, RIGHT, PEER_RIGHT, FWD_RIGHT, c, peer)

    def pair(side, slot, first, count, own=False, fresh=False):
        block = z[side, slot, pl.ds(first, count)]
        logits = scale * dot(z[1 - side, OWN], block, ((1,), (1,))) + shift
        coef = 1.0 / (1.0 + jnp.exp(-logits))
        if own:
            same = lax.broadcasted_iota(jnp.int32, coef.shape, 0) == (
                lax.broadcasted_iota(jnp.int32, coef.shape, 1) + first
            )
            coef = jnp.where(same, coef - 1.0, coef)
        term = dot(coef.astype(BF), block, ((1,), (0,)))
        g[...] = term if fresh else g[...] + term

    def halves(side, h):
        for slot in (LEFT, RIGHT, PEER_LEFT, PEER_RIGHT):
            if slot in (PEER_LEFT, PEER_RIGHT):
                for c in range(h * CH // 2, (h + 1) * CH // 2):
                    await_block(side, slot, c)
            pair(side, slot, h * ROWS // 2, ROWS // 2)

    def make_du(side):
        def rows(i, _):
            at_rows = pl.ds(pl.multiple_of(i * STRIP, STRIP), STRIP)
            grad = g[at_rows] * scale
            u = unit[side, at_rows]
            inner = jnp.sum(u * grad, axis=1, keepdims=True)
            du[side, at_rows] = ((grad - u * inner) * inv[side, at_rows]).astype(BF)
            return 0

        lax.fori_loop(0, ROWS // STRIP, rows, 0)

    def make_demb(side, out, sem):
        demb[side] = dot(du[side], proj[side], ((1,), (1,))).astype(BF)
        copy = pltpu.make_async_copy(demb.at[side], out, sem)
        copy.start()
        return copy

    def sum_steps(side, order):
        mine = pl.ds(pl.multiple_of(core * HALF, HALF), HALF)
        theirs = pl.ds(pl.multiple_of((1 - core) * HALF, HALF), HALF)
        cols = [pl.ds(p * PCOLS, PCOLS) for p in range(PARTS)]

        def quarter(i):
            return pl.ds(pl.multiple_of(i * QROWS, QROWS), QROWS)

        def own_rows(i):
            return pl.ds(pl.multiple_of(core * HALF + i * QROWS, QROWS), QROWS)

        def to_peer():
            for p in range(PARTS):
                dmat[side, :, cols[p]] = dot(
                    emb[side], du[side, :, cols[p]], ((0,), (0,))
                ).astype(BF)
                send(
                    dmat.at[side, theirs, cols[p]], half.at[side, :, cols[p]],
                    s0s.at[side, p], s0r.at[side, p], peer,
                )

        def first_axis():
            for p in range(PARTS):
                await_recv(half.at[side, :, cols[p]], s0r.at[side, p])
                half[side, :, cols[p]] = (
                    half[side, :, cols[p]].astype(F32) + dmat[side, mine, cols[p]].astype(F32)
                ).astype(BF)
                axis = order[p][0]
                for d in (1, 2, 3):
                    send(
                        half.at[side, quarter(lax.rem(at[axis] + d, 4)), cols[p]],
                        r1.at[side, p, d - 1],
                        s1s.at[side, p, d - 1], s1r.at[side, p, d - 1], axis_peer(axis, d),
                    )

        def second_axis():
            for p in range(PARTS):
                for d in range(3):
                    await_recv(r1.at[side, p, d], s1r.at[side, p, d])
                total = half[side, quarter(at[order[p][0]]), cols[p]].astype(F32)
                for d in range(3):
                    total = total + r1[side, p, d].astype(F32)
                total = total.astype(BF)
                for t in range(TILES):
                    r, c = divmod(t, PCOLS // 128)
                    p2[side, p, t // PIECE, pl.ds(t % PIECE * 16, 16)] = total[
                        r * 16 : r * 16 + 16, c * 128 : c * 128 + 128
                    ]
                for t in range(TILES, 4 * PIECE):
                    p2[side, p, t // PIECE, pl.ds(t % PIECE * 16, 16)] = jnp.zeros((16, 128), BF)
                axis = order[p][1]
                for d in (1, 2, 3):
                    send(
                        p2.at[side, p, lax.rem(at[axis] + d, 4)], r2.at[side, p, d - 1],
                        s2s.at[side, p, d - 1], s2r.at[side, p, d - 1], axis_peer(axis, d),
                    )

        def third_axis():
            for p in range(PARTS):
                for d in range(3):
                    await_recv(r2.at[side, p, d], s2r.at[side, p, d])
                total = p2[side, p, at[order[p][1]]].astype(F32)
                for d in range(3):
                    total = total + r2[side, p, d].astype(F32)
                axis = order[p][2]
                x3[side, p, at[axis]] = total.astype(BF)
                for d in (1, 2, 3):
                    send(
                        x3.at[side, p, at[axis]], x3.at[side, p, at[axis]],
                        s3s.at[side, p, d - 1], s3r.at[side, p, d - 1], axis_peer(axis, d),
                    )

        def second_back():
            for p in range(PARTS):
                axis = order[p][2]
                for d in (1, 2, 3):
                    await_recv(x3.at[side, p, lax.rem(at[axis] + 4 - d, 4)], s3r.at[side, p, d - 1])
                total = x3[side, p, 0].astype(F32)
                for i in (1, 2, 3):
                    total = total + x3[side, p, i].astype(F32)
                axis = order[p][1]
                a2[side, p, at[axis]] = total.astype(BF)
                for d in (1, 2, 3):
                    send(
                        a2.at[side, p, at[axis]], a2.at[side, p, at[axis]],
                        a2s.at[side, p, d - 1], a2r.at[side, p, d - 1], axis_peer(axis, d),
                    )

        def first_back():
            for p in range(PARTS):
                axis = order[p][1]
                for d in (1, 2, 3):
                    await_recv(a2.at[side, p, lax.rem(at[axis] + 4 - d, 4)], a2r.at[side, p, d - 1])
                axis = order[p][0]
                for t in range(TILES):
                    r, c = divmod(t, PCOLS // 128)
                    full[
                        side,
                        pl.ds(pl.multiple_of(core * HALF + at[axis] * QROWS + r * 16, 16), 16),
                        pl.ds(p * PCOLS + c * 128, 128),
                    ] = a2[side, p, t // PIECE, pl.ds(t % PIECE * 16, 16)]
                piece = full.at[side, own_rows(at[axis]), cols[p]]
                for d in (1, 2, 3):
                    send(piece, piece, a1s.at[side, p, d - 1], a1r.at[side, p, d - 1], axis_peer(axis, d))
                send(piece, piece, fs.at[side, p, 0], fr.at[side, p, 0], peer)

        def peer_back():
            for p in range(PARTS):
                axis = order[p][0]
                for d in (1, 2, 3):
                    piece = full.at[side, own_rows(lax.rem(at[axis] + 4 - d, 4)), cols[p]]
                    await_recv(piece, a1r.at[side, p, d - 1])
                    send(piece, piece, fs.at[side, p, d], fr.at[side, p, d], peer)

        def finish():
            for p in range(PARTS):
                axis = order[p][0]
                for d in range(4):
                    piece = full.at[
                        side,
                        pl.ds(
                            pl.multiple_of(
                                (1 - core) * HALF + lax.rem(at[axis] + 4 - d, 4) * QROWS, QROWS
                            ),
                            QROWS,
                        ),
                        cols[p],
                    ]
                    await_recv(piece, fr.at[side, p, d])

        return [
            to_peer, first_axis, second_axis, third_axis, second_back, first_back, peer_back, finish
        ]

    loads[0].wait()
    loads[1].wait()
    for load in loads[2:]:
        load.start()
    for h in (0, 1):
        make_unit(0, h * ROWS // 2, ROWS // 2)
        if h == 0:
            pl.semaphore_wait(barrier, len(friends))
        for c in range(h * CH // 2, (h + 1) * CH // 2):
            send_own(0, c)
    loads[2].wait()
    loads[3].wait()
    make_unit(1)

    def finish_side(side):
        target = 1 - side
        make_du(target)
        steps = sum_steps(target, AXES[side])
        steps[0]()
        return steps

    def put_demb(side):
        outs.append(make_demb(1 - side, (die_hbm, dte_hbm)[side], out_sem.at[side]))

    def own_pair(side):
        for h in (0, 1):
            pair(side, OWN, h * ROWS // 2, ROWS // 2, own=True, fresh=h == 0)

    def peer_pair(side):
        for c in range(CH):
            await_block(side, PEER, c)
        pair(side, PEER, 0, ROWS)

    def far_pair(side):
        for h in (0, 1):
            for c in range(h * CH // 2, (h + 1) * CH // 2):
                await_block(side, FAR, c)
            pair(side, FAR, h * ROWS // 2, ROWS // 2)

    def put_out(target, out, sem):
        outs.append(pltpu.make_async_copy(full.at[target], out, sem))
        outs[-1].start()

    outs = []
    own_pair(0)
    peer_pair(0)
    forward(0, 0)
    forward(0, 1)
    halves(0, 0)
    forward(0, 2)
    forward(0, 3)
    for c in range(CH):
        send_own(1, c)
    halves(0, 1)
    far_pair(0)
    image = finish_side(0)
    own_pair(1)
    peer_pair(1)
    put_demb(0)
    forward(1, 0)
    forward(1, 1)
    forward(1, 2)
    forward(1, 3)
    image[1]()
    halves(1, 0)
    halves(1, 1)
    far_pair(1)
    text = finish_side(1)
    image[2]()
    text[1]()
    put_demb(1)
    image[3]()
    text[2]()
    image[4]()
    text[3]()
    image[5]()
    text[4]()
    image[6]()
    text[5]()
    image[7]()
    put_out(1, dip_hbm, out_sem.at[2])
    text[6]()
    text[7]()
    put_out(0, dtp_hbm, out_sem.at[3])
    for out in outs:
        out.wait()
    for copy in started:
        copy.wait_send()


def finish_kernel(ie, te, ip, tp, out_ie, out_te, out_ip, out_tp, narrow, wide, embs, sems):
    emb_ins = [
        pltpu.make_async_copy(src, embs.at[i], sems.at[2, i]) for i, src in enumerate((ie, te))
    ]
    emb_backs = [
        pltpu.make_async_copy(embs.at[i], dst, sems.at[2, 2 + i])
        for i, dst in enumerate((out_ie, out_te))
    ]
    pieces = [
        (m, src, dst, pl.ds(c * PIECE_ROWS, PIECE_ROWS), c)
        for c in range(D // PIECE_ROWS)
        for m, (src, dst) in enumerate(((ip, out_ip), (tp, out_tp)))
    ]
    ins = [
        pltpu.make_async_copy(src.at[rows], narrow.at[m, rows], sems.at[m, c])
        for m, src, dst, rows, c in pieces
    ]
    backs = [
        pltpu.make_async_copy(wide.at[m, rows], dst.at[rows], sems.at[3 + m, c])
        for m, src, dst, rows, c in pieces
    ]
    for copy in ins + emb_ins:
        copy.start()
    for (m, src, dst, rows, c), copy, back in zip(pieces, ins, backs):
        copy.wait()
        wide[m, rows] = narrow[m, rows].astype(F32)
        back.start()
    for copy, back in zip(emb_ins, emb_backs):
        copy.wait()
        back.start()
    for copy in backs + emb_backs:
        copy.wait()


def finish(*parts):
    anywhere = pl.BlockSpec(memory_space=pl.ANY)
    return pl.pallas_call(
        finish_kernel,
        out_shape=tuple(
            jax.ShapeDtypeStruct((n, D), kind) for n, kind in ((ROWS, BF), (ROWS, BF), (D, F32), (D, F32))
        ),
        in_specs=[anywhere] * 4,
        out_specs=(anywhere,) * 4,
        scratch_shapes=[
            pltpu.VMEM((2, D, D), BF),
            pltpu.VMEM((2, D, D), F32),
            pltpu.VMEM((2, ROWS, D), BF),
            pltpu.SemaphoreType.DMA((5, D // PIECE_ROWS)),
        ],
        compiler_params=pltpu.CompilerParams(vmem_limit_bytes=62 << 20),
        name="finish",
    )(*parts)


def body(img_emb, txt_emb, img_proj, txt_proj, log_scale, bias):
    any_space = pl.BlockSpec(memory_space=pl.ANY)
    smem = pl.BlockSpec(memory_space=pltpu.SMEM)
    dma = pltpu.SemaphoreType.DMA
    d_img_emb, d_txt_emb, d_img_proj, d_txt_proj = pl.pallas_call(
        kernel,
        out_shape=(
            jax.ShapeDtypeStruct((ROWS, D), BF),
            jax.ShapeDtypeStruct((ROWS, D), BF),
            jax.ShapeDtypeStruct((D, D), BF),
            jax.ShapeDtypeStruct((D, D), BF),
        ),
        in_specs=[smem, smem] + [any_space] * 4,
        out_specs=(any_space,) * 4,
        scratch_shapes=[
            pltpu.VMEM((2, ROWS, D), BF),
            pltpu.VMEM((2, D, D), BF),
            pltpu.VMEM((2, 7, ROWS, D), BF),
            pltpu.VMEM((2, ROWS, D), F32),
            pltpu.VMEM((2, ROWS, 1), F32),
            pltpu.VMEM((ROWS, D), F32),
            pltpu.VMEM((2, ROWS, D), BF),
            pltpu.VMEM((2, ROWS, D), BF),
            pltpu.VMEM((2, D, D), BF),
            pltpu.VMEM((2, HALF, D), BF),
            pltpu.VMEM((2, PARTS, 3, QROWS, PCOLS), BF),
            pltpu.VMEM((2, PARTS, 4, PIECE * 16, 128), BF),
            pltpu.VMEM((2, PARTS, 3, PIECE * 16, 128), BF),
            pltpu.VMEM((2, PARTS, 4, PIECE * 16, 128), BF),
            pltpu.VMEM((2, PARTS, 4, PIECE * 16, 128), BF),
            pltpu.VMEM((2, D, D), BF),
            dma((4,)), dma((4,)),
            dma((2, 6, CH)), dma((2, 7, CH)),
            dma((2, PARTS)), dma((2, PARTS)),
            dma((2, PARTS, 3)), dma((2, PARTS, 3)),
            dma((2, PARTS, 3)), dma((2, PARTS, 3)),
            dma((2, PARTS, 3)), dma((2, PARTS, 3)),
            dma((2, PARTS, 3)), dma((2, PARTS, 3)),
            dma((2, PARTS, 3)), dma((2, PARTS, 3)),
            dma((2, PARTS, 4)), dma((2, PARTS, 4)),
        ],
        compiler_params=pltpu.CompilerParams(
            collective_id=0, has_side_effects=True, vmem_limit_bytes=62 << 20
        ),
        name="band_gradients",
    )(log_scale, bias, img_emb, txt_emb, img_proj, txt_proj)
    return finish(d_img_emb, d_txt_emb, d_img_proj, d_txt_proj)


def solution(mesh):
    return jax.shard_map(
        body,
        mesh=mesh,
        in_specs=(P("dp", None), P("dp", None), P(), P(), P(), P()),
        out_specs=(P("dp", None), P("dp", None), P(), P()),
        check_vma=False,
    )
```
